32 devices in a mesh: adapter: 8 (over z, y), tensor: 4 (over x, core).
Axes of the slice: x: 2, y: 2, z: 4, core: 2. Of those that a mesh axis runs over, the one named last changes fastest.
Arguments:
- partials: bfloat16 [4, 512, 8192], P('tensor', 'adapter'), may hold values from -4 to 4
- residual: bfloat16 [512, 8192], P('adapter'), may hold values from -80 to 80
- attention_norm_gain: bfloat16 [8192], replicated, may hold values from 0.25 to 1.75
- key_value_weight: bfloat16 [8192, 8, 256], P(None, 'tensor'), may hold values from -0.0625 to 0.0625
- adapter_down_weight: bfloat16 [8192, 8192], P('tensor', 'adapter'), may hold values from -0.0625 to 0.0625
- adapter_up_weight: bfloat16 [8192, 8, 256], P('adapter', 'tensor'), may hold values from -0.75 to 0.75
- row_adapter_index: int32 [512], P('adapter'), may hold values from 0 to 127, as said below
- queries: bfloat16 [512, 8192], P('adapter', 'tensor'), may hold values from -10 to 10
- key_value_cache: bfloat16 [64, 2, 1024, 1024], P('adapter', None, None, 'tensor'), may hold values from -10 to 10
- prompt_cache_length: int32 [64], P('adapter'), may hold values from 2 to 1024
Outputs:
- hidden_out: bfloat16 [512, 8192], P('adapter', 'tensor')
- new_kv: bfloat16 [512, 8, 256], P('adapter', 'tensor')
- attn_out: bfloat16 [512, 8192], P('adapter', 'tensor')
The draws below stay inside these ranges and needn't reach their ends.
Inputs may be any that keep to these rules, and one draw needn't show every extreme that they name: `row_adapter_index`: adapter g is held by index g // 16 of the adapter axis. Of the 64 rows on one index of the adapter axis at most 32 use adapters held by one index; in every draw one index receives exactly 32 rows from every index.
All inputs are finite; a program needn't handle non-finite values.
Results may differ from the reference program's by a relative error of at most 0.012.
Values may be sent and summed in bfloat16 or wider, within the bound.
A program may use at most 128 MiB of HBM per device.

```python
import math
import jax
import jax.numpy as jnp
from jax import lax

MODEL_DIM = 8192
HEADS = 64
KEY_VALUE_HEADS = 8
HEAD_SIZE = 128
ADAPTER_RANK = 64
FAN = 8
CACHE = 1024
ADAPT_DEV = 16
ROW_DEV = 64
PROMPTS = 64
ROWS = 512
ADAPTER_TOTAL = 128
CAP = 32
N_TENSOR = 4


def draw_residual(key, part):
    noise_key, row_key, column_key = jax.random.split(key, 3)
    noise_draw = jnp.clip(jax.random.normal(noise_key, (ROWS, MODEL_DIM), jnp.float32), -4.0, 4.0)
    row_scale = jnp.exp(jax.random.uniform(row_key, (ROWS, 1), jnp.float32, math.log(0.25), math.log(2.5)))
    column_scale = jnp.exp(jax.random.uniform(column_key, (1, MODEL_DIM), jnp.float32, math.log(0.25), math.log(2.5)))
    position = jnp.arange(MODEL_DIM, dtype=jnp.float32)[None, :] / MODEL_DIM
    rise_factor = jnp.sqrt(1.0 + 6.0 * position)
    values = noise_draw * row_scale * column_scale * rise_factor
    return values.astype(jnp.bfloat16)


def draw_queries(key, part):
    draw_key = jax.random.fold_in(key, 1)
    values = jnp.clip(jax.random.normal(draw_key, (ROWS, HEADS * HEAD_SIZE), jnp.float32), -6.0, 6.0)
    return values.astype(jnp.bfloat16)


def draw_key_value_cache(key, part):
    draw_key = jax.random.fold_in(key, 2)
    shape_full = (PROMPTS, 2, CACHE, KEY_VALUE_HEADS * HEAD_SIZE)
    values = jnp.clip(jax.random.normal(draw_key, shape_full, jnp.float32), -6.0, 6.0)
    return values.astype(jnp.bfloat16)


def draw_row_adapter_index(key, part):
    owners = ADAPTER_TOTAL // ADAPT_DEV
    hot_key, perm_key, local_key = jax.random.split(key, 3)
    hot_owner = jax.random.randint(hot_key, (), 0, owners)
    candidates = (owners - 1) * CAP

    def one_block(block_key):
        choose_key, shuffle_key = jax.random.split(block_key)
        chosen = jax.random.permutation(choose_key, candidates)[:ROW_DEV - CAP]
        others = (chosen // CAP).astype(jnp.int32)
        others = others + (others >= hot_owner).astype(jnp.int32)
        owner_list = jnp.concatenate([jnp.full((CAP,), hot_owner, jnp.int32), others])
        return jax.random.permutation(shuffle_key, owner_list)
    owner_rows = jax.vmap(one_block)(jax.random.split(perm_key, owners)).reshape(ROWS)
    local_pick = jax.random.randint(local_key, (ROWS,), 0, ADAPT_DEV)
    return (owner_rows * ADAPT_DEV + local_pick).astype(jnp.int32)


def draw_prompt_cache_length(key, part):
    first_key, second_key, full_key = jax.random.split(key, 3)
    first_draw = jax.random.randint(first_key, (PROMPTS,), 0, CACHE - 1)
    second_draw = jax.random.randint(second_key, (PROMPTS,), 1, CACHE + 1)
    lengths = 2 + first_draw * second_draw // CACHE
    full_prompt = jax.random.randint(full_key, (), 0, PROMPTS)
    lengths = jnp.where(jnp.arange(PROMPTS) == full_prompt, CACHE, lengths)
    return lengths.astype(jnp.int32)


def block_levels(stream_key, extent, shards, smallest, largest):
    factor_of, own = 1.0, jax.random.fold_in(stream_key, 6)
    for dim, parts in shards:
        heights = jnp.exp(jax.random.uniform(jax.random.fold_in(own, dim), (parts,), jnp.float32, smallest / len(shards), largest / len(shards)))
        factor_of = factor_of * jnp.repeat(heights, extent[dim] // parts).reshape([-1 if axis == dim else 1 for axis in range(len(extent))])
    return factor_of


def normal_values(stream_key, dims, deviation, reach, cuts=(), kind=jnp.bfloat16):
    array = jax.random.normal(stream_key, dims, jnp.float32) * deviation
    if len(cuts) > 0:
        array = block_levels(stream_key, dims, cuts, -0.22, 0.18) * array
    return jnp.clip(array, min=-reach, max=reach).astype(kind)


def setup_inputs(seed: int = 0) -> dict:
    splits = jax.random.split(jax.random.key(seed), 11)
    partials = normal_values(splits[0], (N_TENSOR, ROWS, MODEL_DIM), 0.3, 4.0, ((0, 4), (1, 8)))
    residual = draw_residual(jax.random.fold_in(splits[10], 71), 0)
    attention_norm_gain = jnp.clip(1.0 + 0.15 * jax.random.normal(splits[2], (MODEL_DIM,), jnp.float32), 0.25, 1.75).astype(jnp.bfloat16)
    key_value_weight = normal_values(splits[3], (MODEL_DIM, KEY_VALUE_HEADS, 2 * HEAD_SIZE), MODEL_DIM ** -0.5, 0.0625, ((1, 4),))
    adapter_down_weight = normal_values(splits[4], (MODEL_DIM, ADAPTER_TOTAL * ADAPTER_RANK), MODEL_DIM ** -0.5, 0.0625, ((0, 4), (1, 8)))
    adapter_up_weight = normal_values(splits[5], (ADAPTER_TOTAL * ADAPTER_RANK, KEY_VALUE_HEADS, 2 * HEAD_SIZE), ADAPTER_RANK ** -0.5, 0.75, ((0, 8), (1, 4)))
    row_adapter_index = draw_row_adapter_index(jax.random.fold_in(splits[10], 71), 0)
    queries = draw_queries(jax.random.fold_in(splits[10], 71), 0)
    key_value_cache = draw_key_value_cache(jax.random.fold_in(splits[10], 71), 0)
    prompt_cache_length = draw_prompt_cache_length(jax.random.fold_in(splits[10], 71), 0)
    return {"partials": partials, "residual": residual, "attention_norm_gain": attention_norm_gain, "key_value_weight": key_value_weight, "adapter_down_weight": adapter_down_weight, "adapter_up_weight": adapter_up_weight, "row_adapter_index": row_adapter_index, "queries": queries, "key_value_cache": key_value_cache, "prompt_cache_length": prompt_cache_length}


EPSILON = 1e-05
ADAPTER_SCALE = 0.5

def reference(partials, residual, attention_norm_gain, key_value_weight, adapter_down_weight, adapter_up_weight, row_adapter_index, queries, key_value_cache, prompt_cache_length):
    summed = residual.astype(jnp.float32) + lax.optimization_barrier(jnp.sum(partials.astype(jnp.float32), axis=0))
    hidden_out = summed.astype(jnp.bfloat16)
    hidden_wide = hidden_out.astype(jnp.float32)
    mean_sq = lax.optimization_barrier(jnp.mean(hidden_wide * hidden_wide, axis=1, keepdims=True))
    normalized_input = (hidden_wide * lax.rsqrt(mean_sq + EPSILON) * attention_norm_gain.astype(jnp.float32)).astype(jnp.bfloat16)
    key_value_width = KEY_VALUE_HEADS * 2 * HEAD_SIZE
    base_kv = jnp.dot(normalized_input, key_value_weight.reshape(MODEL_DIM, key_value_width), preferred_element_type=jnp.float32)
    flattened_up = adapter_up_weight.reshape(ADAPTER_TOTAL * ADAPTER_RANK, key_value_width)

    def adapter_row(prompt_entry):
        normed_row, adapter_id = prompt_entry
        offset_index = (adapter_id * ADAPTER_RANK).astype(jnp.int32)
        down_weight_block = lax.dynamic_slice_in_dim(adapter_down_weight, offset_index, ADAPTER_RANK, 1)
        reduced_rank_rows = jnp.dot(normed_row[None, :], down_weight_block, preferred_element_type=jnp.float32).astype(jnp.bfloat16)
        up_weight_block = lax.dynamic_slice_in_dim(flattened_up, offset_index, ADAPTER_RANK, 0)
        return (ADAPTER_SCALE * jnp.dot(reduced_rank_rows, up_weight_block, preferred_element_type=jnp.float32)).astype(jnp.bfloat16)[0]
    update_rows = lax.map(adapter_row, (normalized_input, row_adapter_index))
    new_kv = (base_kv + update_rows.astype(jnp.float32)).astype(jnp.bfloat16).reshape(ROWS, KEY_VALUE_HEADS, 2 * HEAD_SIZE)
    group_size = HEADS // KEY_VALUE_HEADS
    score_scale = HEAD_SIZE ** (-0.5)
    query_heads = queries.reshape(PROMPTS, FAN, KEY_VALUE_HEADS, group_size, HEAD_SIZE)
    new_heads = new_kv.reshape(PROMPTS, FAN, KEY_VALUE_HEADS, 2 * HEAD_SIZE)
    cache_heads = key_value_cache.reshape(PROMPTS, 2, CACHE, KEY_VALUE_HEADS, HEAD_SIZE)

    def attend_prompt(prompt_entry):
        query_block, cache_block, length, new_block = prompt_entry
        query_wide = query_block.astype(jnp.float32)
        cache_keys = cache_block[0].astype(jnp.float32)
        cache_values = cache_block[1].astype(jnp.float32)
        scores = jnp.einsum('fkgd,ckd->fkgc', query_wide, cache_keys) * score_scale
        valid_mask = jnp.arange(CACHE) < length
        scores = jnp.where(valid_mask, scores, -jnp.inf)
        own_key = new_block[:, :, :HEAD_SIZE].astype(jnp.float32)
        own_value = new_block[:, :, HEAD_SIZE:].astype(jnp.float32)
        own_score = jnp.einsum('fkgd,fkd->fkg', query_wide, own_key) * score_scale
        score_top = jnp.maximum(lax.optimization_barrier(jnp.max(scores, axis=-1)), own_score)
        weights_low = jnp.exp(scores - score_top[:, :, :, None]).astype(jnp.bfloat16)
        weights = lax.optimization_barrier(weights_low).astype(jnp.float32)
        own_low = jnp.exp(own_score - score_top).astype(jnp.bfloat16)
        own_weight = lax.optimization_barrier(own_low).astype(jnp.float32)
        weight_total = lax.optimization_barrier(jnp.sum(weights, axis=-1)) + own_weight
        weighted = jnp.einsum('fkgc,ckd->fkgd', weights, cache_values) + own_weight[:, :, :, None] * own_value[:, :, None, :]
        return (weighted / weight_total[:, :, :, None]).astype(jnp.bfloat16)
    attended = lax.map(attend_prompt, (query_heads, cache_heads, prompt_cache_length, new_heads))
    attn_out = attended.reshape(ROWS, HEADS * HEAD_SIZE)
    return (hidden_out, new_kv, attn_out)
```

```python
import functools

import jax
import jax.numpy as jnp
from jax import lax
from jax.experimental import pallas as pl
from jax.experimental.pallas import tpu as pltpu
from jax.sharding import PartitionSpec as P

HEAD_SIZE = 128
ADAPTER_RANK = 64
FAN = 8
EPSILON = 1e-05
ADAPTER_SCALE = 0.5
MESH = pl.DeviceIdType.MESH
F32 = jnp.float32
BF16 = jnp.bfloat16
SCALE = HEAD_SIZE ** (-0.5)


def cache_kernel(lengths, q_ref, kv_ref, acc_ref, top_ref, total_ref):
    length = lengths[pl.program_id(0)]
    kv_heads = kv_ref.shape[3] // HEAD_SIZE
    group = q_ref.shape[1] // HEAD_SIZE // kv_heads
    q = q_ref[...].astype(F32)
    lane = lax.broadcasted_iota(jnp.int32, (FAN, 128), 1)
    tops = jnp.zeros((FAN, 128), F32)
    totals = jnp.zeros((FAN, 128), F32)
    for k in range(kv_heads):
        cols = slice(k * HEAD_SIZE, (k + 1) * HEAD_SIZE)
        stack = jnp.concatenate(
            [q[:, (k * group + g) * HEAD_SIZE:(k * group + g + 1) * HEAD_SIZE] for g in range(group)], axis=0
        ).astype(BF16)
        scores = lax.dot_general(
            stack, kv_ref[0, 0, :, cols], (((1,), (1,)), ((), ())), preferred_element_type=F32
        ) * SCALE
        slot = lax.broadcasted_iota(jnp.int32, scores.shape, 1)
        scores = jnp.where(slot < length, scores, -jnp.inf)
        top = jnp.max(scores, axis=1, keepdims=True)
        weights = jnp.exp(scores - top).astype(BF16)
        total = jnp.sum(weights.astype(F32), axis=1, keepdims=True)
        acc = jnp.dot(weights, kv_ref[0, 1, :, cols], preferred_element_type=F32)
        for g in range(group):
            h = k * group + g
            rows = slice(g * FAN, (g + 1) * FAN)
            acc_ref[:, h * HEAD_SIZE:(h + 1) * HEAD_SIZE] = acc[rows]
            tops = jnp.where(lane == h, top[rows], tops)
            totals = jnp.where(lane == h, total[rows], totals)
    top_ref[...] = tops
    total_ref[...] = totals


def attend_cache(queries, cache, lengths):
    prompts, _, slots, width = cache.shape
    rows, q_width = queries.shape
    return pl.pallas_call(
        cache_kernel,
        out_shape=(
            jax.ShapeDtypeStruct((rows, q_width), F32),
            jax.ShapeDtypeStruct((rows, 128), F32),
            jax.ShapeDtypeStruct((rows, 128), F32),
        ),
        grid_spec=pltpu.PrefetchScalarGridSpec(
            num_scalar_prefetch=1,
            grid=(prompts,),
            in_specs=[
                pl.BlockSpec((FAN, q_width), lambda p, n: (p, 0)),
                pl.BlockSpec((1, 2, slots, width), lambda p, n: (p, 0, 0, 0)),
            ],
            out_specs=(
                pl.BlockSpec((FAN, q_width), lambda p, n: (p, 0)),
                pl.BlockSpec((FAN, 128), lambda p, n: (p, 0)),
                pl.BlockSpec((FAN, 128), lambda p, n: (p, 0)),
            ),
        ),
        compiler_params=pltpu.CompilerParams(vmem_limit_bytes=16 * 2**20),
        cost_estimate=pl.CostEstimate(
            flops=4 * rows * q_width * slots, bytes_accessed=2 * cache.size + 4 * rows * q_width,
            transcendentals=rows * q_width // HEAD_SIZE * slots,
        ),
    )(lengths, queries, cache)


W_CHUNKS = 4


def rows_kernel(
    adapters, tensors, cap,
    hidden_ref, gain_ref, weight_hbm, down_hbm, up_ref, pick_ref, place_ref, ids_ref,
    q_ref, acc_ref, top_ref, total_ref,
    new_kv_ref, attn_ref,
    weight, down, normed, out_rows, in_rows, low_out, low_in, delta, back, base,
    weight_sem, down_sem, row_send, row_recv, low_send, low_recv, back_send, back_recv,
):
    a = lax.axis_index("adapter")
    t = lax.axis_index("tensor")
    rows, width = hidden_ref.shape
    chunk = width // W_CHUNKS
    quarter = width // tensors
    slots = adapters * cap

    loads = [
        pltpu.make_async_copy(
            weight_hbm.at[pl.ds(i * chunk, chunk)], weight.at[pl.ds(i * chunk, chunk)], weight_sem.at[i]
        )
        for i in range(W_CHUNKS)
    ]
    for load in loads:
        load.start()
    load_down = pltpu.make_async_copy(down_hbm, down, down_sem)
    load_down.start()

    barrier = pltpu.get_barrier_semaphore()

    def greet_adapter(d, carry):
        pl.semaphore_signal(barrier, inc=1, device_id=(lax.rem(a + d, adapters), t), device_id_type=MESH)
        return carry

    lax.fori_loop(1, adapters, greet_adapter, 0)
    for d in range(1, tensors):
        pl.semaphore_signal(barrier, inc=1, device_id=(a, lax.rem(t + d, tensors)), device_id_type=MESH)

    square = jnp.zeros((rows, 128), F32)
    for i in range(W_CHUNKS):
        part = hidden_ref[:, i * chunk:(i + 1) * chunk].astype(F32)
        part = part * part
        for j in range(chunk // 128):
            square = square + part[:, j * 128:(j + 1) * 128]
    inverse = lax.rsqrt(jnp.sum(square, axis=1, keepdims=True) / width + EPSILON)
    for i in range(W_CHUNKS):
        cols = slice(i * chunk, (i + 1) * chunk)
        normed[:, cols] = (
            hidden_ref[:, cols].astype(F32) * inverse * gain_ref[:, cols].astype(F32)
        ).astype(BF16)

    mine = normed[:, pl.ds(pl.multiple_of(t * quarter, quarter), quarter)]
    out_rows[...] = jnp.dot(pick_ref[...], mine, preferred_element_type=F32).astype(BF16).reshape(out_rows.shape)

    pl.semaphore_wait(barrier, adapters - 1 + tensors - 1)

    def row_copy(d):
        other = lax.rem(a + d, adapters)
        return pltpu.make_async_remote_copy(
            src_ref=out_rows.at[other], dst_ref=in_rows.at[a], send_sem=row_send.at[d],
            recv_sem=row_recv.at[adapters - d], device_id=(other, t), device_id_type=MESH,
        )

    def back_copy(d):
        other = lax.rem(a + d, adapters)
        return pltpu.make_async_remote_copy(
            src_ref=delta.at[other], dst_ref=back.at[a], send_sem=back_send.at[d],
            recv_sem=back_recv.at[adapters - d], device_id=(other, t), device_id_type=MESH,
        )

    def row_arrival(d):
        other = lax.rem(a + d, adapters)
        return pltpu.make_async_remote_copy(
            src_ref=out_rows.at[other], dst_ref=in_rows.at[other], send_sem=row_send.at[d],
            recv_sem=row_recv.at[d], device_id=(other, t), device_id_type=MESH,
        )

    def back_arrival(d):
        other = lax.rem(a + d, adapters)
        return pltpu.make_async_remote_copy(
            src_ref=delta.at[other], dst_ref=back.at[other], send_sem=back_send.at[d],
            recv_sem=back_recv.at[d], device_id=(other, t), device_id_type=MESH,
        )

    def each(function):
        def step(d, carry):
            function(d)
            return carry

        lax.fori_loop(1, adapters, step, 0)

    each(lambda d: row_copy(d).start())
    in_rows[a] = out_rows[a]

    for i in range(W_CHUNKS):
        loads[i].wait()
        part = jnp.dot(
            normed[:, i * chunk:(i + 1) * chunk], weight[i * chunk:(i + 1) * chunk, :], preferred_element_type=F32
        )
        base[...] = part if i == 0 else base[...] + part
    load_down.wait()

    each(lambda d: row_arrival(d).wait_recv())

    lane = lax.broadcasted_iota(jnp.int32, (slots, 128), 1)
    odd = jnp.where(lane >= ADAPTER_RANK, 1, 0)
    ids = ids_ref[...] - odd
    got = in_rows[...].reshape(slots, quarter)
    low = jnp.zeros((slots, 128), F32)
    wide = 2
    for j in range(0, down.shape[1] // 128, wide):
        part = jnp.dot(got, down[:, j * 128:(j + wide) * 128], preferred_element_type=F32)
        for i in range(wide):
            low = low + jnp.where(ids == 2 * (j + i), part[:, i * 128:(i + 1) * 128], 0.0)
    low_out[...] = low.astype(BF16)

    shares = []
    for d in range(1, tensors):
        other = lax.rem(t + d, tensors)
        share = pltpu.make_async_remote_copy(
            src_ref=low_out, dst_ref=low_in.at[tensors - d], send_sem=low_send.at[d],
            recv_sem=low_recv.at[tensors - d], device_id=(a, other), device_id_type=MESH,
        )
        share.start()
        shares.append(share)
    for share in shares:
        share.wait()
    for d in range(1, tensors):
        low = low + low_in[d].astype(F32)
    low = low.astype(BF16).astype(F32)

    spread = jnp.concatenate(
        [jnp.where(ids == 2 * j, low, 0.0).astype(BF16) for j in range(down.shape[1] // 128)], axis=1
    )
    delta[...] = (
        ADAPTER_SCALE * jnp.dot(spread, up_ref[...], preferred_element_type=F32)
    ).astype(BF16).reshape(delta.shape)
    each(lambda d: back_copy(d).start())
    back[a] = delta[a]
    each(lambda d: back_arrival(d).wait_recv())

    update = jnp.dot(place_ref[...], back[...].reshape(slots, -1), preferred_element_type=F32)
    new_kv = (base[...] + update).astype(BF16)
    new_kv_ref[...] = new_kv

    kv_heads = new_kv.shape[1] // (2 * HEAD_SIZE)
    group = q_ref.shape[1] // HEAD_SIZE // kv_heads
    for k in range(kv_heads):
        key = new_kv[:, 2 * k * HEAD_SIZE:(2 * k + 1) * HEAD_SIZE].astype(F32)
        value = new_kv[:, (2 * k + 1) * HEAD_SIZE:(2 * k + 2) * HEAD_SIZE].astype(F32)
        for g in range(group):
            h = k * group + g
            cols = slice(h * HEAD_SIZE, (h + 1) * HEAD_SIZE)
            own = jnp.sum(q_ref[:, cols].astype(F32) * key, axis=1, keepdims=True) * SCALE
            cache_top = top_ref[:, h:h + 1]
            top = jnp.maximum(cache_top, own)
            shrink = jnp.exp(cache_top - top)
            weight_own = jnp.exp(own - top).astype(BF16).astype(F32)
            attn_ref[:, cols] = (
                (acc_ref[:, cols] * shrink + weight_own * value)
                / (total_ref[:, h:h + 1] * shrink + weight_own)
            ).astype(BF16)

    each(lambda d: row_copy(d).wait_send())
    each(lambda d: back_copy(d).wait_send())


def finish_rows(
    adapters, tensors, cap, hidden, gain, weight, down, up, pick, place, ids, queries, acc, top, total
):
    rows, width = hidden.shape
    columns = weight.shape[1]
    slots = adapters * cap
    quarter = width // tensors
    vmem = pl.BlockSpec(memory_space=pltpu.VMEM)
    hbm = pl.BlockSpec(memory_space=pl.ANY)
    dma = pltpu.SemaphoreType.DMA
    return pl.pallas_call(
        functools.partial(rows_kernel, adapters, tensors, cap),
        out_shape=(
            jax.ShapeDtypeStruct((rows, columns), BF16),
            jax.ShapeDtypeStruct(queries.shape, BF16),
        ),
        in_specs=[vmem, vmem, hbm, hbm, vmem, vmem, vmem, vmem, vmem, vmem, vmem, vmem],
        out_specs=(vmem, vmem),
        scratch_shapes=[
            pltpu.VMEM(weight.shape, BF16),
            pltpu.VMEM(down.shape, BF16),
            pltpu.VMEM((rows, width), BF16),
            pltpu.VMEM((adapters, cap, quarter), BF16),
            pltpu.VMEM((adapters, cap, quarter), BF16),
            pltpu.VMEM((slots, 128), BF16),
            pltpu.VMEM((tensors, slots, 128), BF16),
            pltpu.VMEM((adapters, cap, columns), BF16),
            pltpu.VMEM((adapters, cap, columns), BF16),
            pltpu.VMEM((rows, columns), F32),
            dma((W_CHUNKS,)),
            dma,
            dma((adapters,)),
            dma((adapters,)),
            dma((tensors,)),
            dma((tensors,)),
            dma((adapters,)),
            dma((adapters,)),
        ],
        compiler_params=pltpu.CompilerParams(
            collective_id=0, has_side_effects=True, vmem_limit_bytes=40 * 2**20
        ),
        cost_estimate=pl.CostEstimate(
            flops=2 * rows * width * columns + 2 * slots * down.size, bytes_accessed=2 * (weight.size + down.size),
            transcendentals=0,
        ),
    )(hidden, gain, weight, down, up, pick, place, ids, queries, acc, top, total)


def per_device(
    partials,
    residual,
    attention_norm_gain,
    key_value_weight,
    adapter_down_weight,
    adapter_up_weight,
    row_adapter_index,
    queries,
    key_value_cache,
    prompt_cache_length,
):
    rows, width = residual.shape
    tensors = lax.axis_size("tensor")
    adapters = lax.axis_size("adapter")
    t = lax.axis_index("tensor")
    a = lax.axis_index("adapter")
    half = width // 2
    core = t % 2
    swap_core = [(i, i ^ 1) for i in range(tensors)]
    swap_chip = [(i, i ^ 2) for i in range(tensors)]

    cap = max(16, 4 * rows // adapters)
    held = adapter_down_weight.shape[1] // ADAPTER_RANK
    every = lax.all_gather(row_adapter_index, "adapter")
    owner = every // held
    order = jnp.arange(rows)
    earlier = (order[None, :] < order[:, None])[None]
    rank = jnp.sum(((owner[:, :, None] == owner[:, None, :]) & earlier).astype(jnp.int32), axis=2)
    slot_ids = jnp.arange(cap)
    here = (owner == a)[:, None, :] & (rank[:, None, :] == slot_ids[None, :, None])
    ids = jnp.sum(jnp.where(here, (every % held)[:, None, :] + 1, 0), axis=2).reshape(-1) - 1
    ids = jnp.broadcast_to(ids[:, None], (adapters * cap, 128))
    own_owner = row_adapter_index // held
    own_rank = jnp.sum(((own_owner[:, None] == own_owner[None, :]) & earlier[0]).astype(jnp.int32), axis=1)
    row_slot = own_owner * cap + own_rank
    slots = jnp.arange(adapters * cap)
    pick = (slots[:, None] == row_slot[None, :]).astype(BF16)
    place = (row_slot[:, None] == slots[None, :]).astype(BF16)

    give = lax.dynamic_slice_in_dim(partials[0], (1 - core) * half, half, 1)
    keep = lax.dynamic_slice_in_dim(partials[0], core * half, half, 1)
    taken = lax.ppermute(give, "tensor", swap_core)
    chip_sum = (keep.astype(F32) + taken.astype(F32)).astype(BF16)
    other_sum = lax.ppermute(chip_sum, "tensor", swap_chip)
    hidden_half = (
        lax.dynamic_slice_in_dim(residual, core * half, half, 1).astype(F32)
        + (chip_sum.astype(F32) + other_sum.astype(F32))
    ).astype(BF16)
    other_half = lax.ppermute(hidden_half, "tensor", swap_core)
    hidden = jnp.where(
        core == 0,
        jnp.concatenate([hidden_half, other_half], axis=1),
        jnp.concatenate([other_half, hidden_half], axis=1),
    )
    quarter = width // tensors
    hidden_part = lax.dynamic_slice_in_dim(hidden, t * quarter, quarter, 1)

    acc, top, total = attend_cache(queries, key_value_cache, prompt_cache_length)
    new_kv, attended = finish_rows(
        adapters, tensors, cap, hidden, attention_norm_gain[None, :],
        key_value_weight.reshape(width, -1), adapter_down_weight,
        adapter_up_weight.reshape(adapter_up_weight.shape[0], -1),
        pick, place, ids, queries, acc, top, total,
    )
    return hidden_part, new_kv.reshape(rows, key_value_weight.shape[1], 2 * HEAD_SIZE), attended


def solution(mesh):
    return jax.shard_map(
        per_device,
        mesh=mesh,
        in_specs=(
            P("tensor", "adapter", None),
            P("adapter", None),
            P(),
            P(None, "tensor", None),
            P("tensor", "adapter"),
            P("adapter", "tensor", None),
            P("adapter"),
            P("adapter", "tensor"),
            P("adapter", None, None, "tensor"),
            P("adapter"),
        ),
        out_specs=(P("adapter", "tensor"), P("adapter", "tensor", None), P("adapter", "tensor")),
        check_vma=False,
    )
```

```python
import functools

import jax
import jax.numpy as jnp
from jax import lax
from jax.experimental import pallas as pl
from jax.experimental.pallas import tpu as pltpu
from jax.sharding import PartitionSpec as P

HEAD_SIZE = 128
ADAPTER_RANK = 64
FAN = 8
EPSILON = 1e-05
ADAPTER_SCALE = 0.5
MESH = pl.DeviceIdType.MESH
F32 = jnp.float32
BF16 = jnp.bfloat16
SCALE = HEAD_SIZE ** (-0.5)


def cache_kernel(lengths, q_ref, kv_ref, acc_ref, top_ref, total_ref):
    length = lengths[pl.program_id(0)]
    slots = kv_ref.shape[2]
    sizes = [slots // 4, slots // 2, slots]
    for i, used in enumerate(sizes):
        above = length > (sizes[i - 1] if i else 0)

        @pl.when(above & (length <= used))
        def attend():
            attend_used(used, length, q_ref, kv_ref, acc_ref, top_ref, total_ref)


def attend_used(used, length, q_ref, kv_ref, acc_ref, top_ref, total_ref):
    kv_heads = kv_ref.shape[3] // HEAD_SIZE
    group = q_ref.shape[1] // HEAD_SIZE // kv_heads
    q = q_ref[...].astype(F32)
    lane = lax.broadcasted_iota(jnp.int32, (FAN, 128), 1)
    tops = jnp.zeros((FAN, 128), F32)
    totals = jnp.zeros((FAN, 128), F32)
    for k in range(kv_heads):
        cols = slice(k * HEAD_SIZE, (k + 1) * HEAD_SIZE)
        stack = jnp.concatenate(
            [q[:, (k * group + g) * HEAD_SIZE:(k * group + g + 1) * HEAD_SIZE] for g in range(group)], axis=0
        ).astype(BF16)
        scores = lax.dot_general(
            stack, kv_ref[0, 0, :used, cols], (((1,), (1,)), ((), ())), preferred_element_type=F32
        ) * SCALE
        slot = lax.broadcasted_iota(jnp.int32, scores.shape, 1)
        scores = jnp.where(slot < length, scores, -jnp.inf)
        top = jnp.max(scores, axis=1, keepdims=True)
        weights = jnp.exp(scores - top).astype(BF16)
        total = jnp.sum(weights.astype(F32), axis=1, keepdims=True)
        acc = jnp.dot(weights, kv_ref[0, 1, :used, cols], preferred_element_type=F32)
        for g in range(group):
            h = k * group + g
            rows = slice(g * FAN, (g + 1) * FAN)
            acc_ref[:, h * HEAD_SIZE:(h + 1) * HEAD_SIZE] = acc[rows]
            tops = jnp.where(lane == h, top[rows], tops)
            totals = jnp.where(lane == h, total[rows], totals)
    top_ref[...] = tops
    total_ref[...] = totals


def attend_cache(queries, cache, lengths):
    prompts, _, slots, width = cache.shape
    rows, q_width = queries.shape
    return pl.pallas_call(
        cache_kernel,
        out_shape=(
            jax.ShapeDtypeStruct((rows, q_width), F32),
            jax.ShapeDtypeStruct((rows, 128), F32),
            jax.ShapeDtypeStruct((rows, 128), F32),
        ),
        grid_spec=pltpu.PrefetchScalarGridSpec(
            num_scalar_prefetch=1,
            grid=(prompts,),
            in_specs=[
                pl.BlockSpec((FAN, q_width), lambda p, n: (p, 0)),
                pl.BlockSpec((1, 2, slots, width), lambda p, n: (p, 0, 0, 0)),
            ],
            out_specs=(
                pl.BlockSpec((FAN, q_width), lambda p, n: (p, 0)),
                pl.BlockSpec((FAN, 128), lambda p, n: (p, 0)),
                pl.BlockSpec((FAN, 128), lambda p, n: (p, 0)),
            ),
        ),
        compiler_params=pltpu.CompilerParams(vmem_limit_bytes=58 * 2**20),
        cost_estimate=pl.CostEstimate(
            flops=4 * rows * q_width * slots, bytes_accessed=2 * cache.size + 4 * rows * q_width,
            transcendentals=rows * q_width // HEAD_SIZE * slots,
        ),
    )(lengths, queries, cache)


W_CHUNKS = 4


def rows_kernel(
    adapters, tensors, cap,
    near_ref, far_ref, gain_ref, weight_hbm, down_hbm, up_ref, pick_ref, place_ref, ids_ref,
    q_ref, acc_ref, top_ref, total_ref,
    new_kv_ref, attn_ref,
    weight, down, normed, out_rows, in_rows, low_out, low_in, delta, back, base,
    weight_sem, down_sem, row_send, row_recv, low_send, low_recv, back_send, back_recv,
):
    a = lax.axis_index("adapter")
    t = lax.axis_index("tensor")
    rows, width = near_ref.shape[0], weight_hbm.shape[0]
    chunk = width // W_CHUNKS
    quarter = width // tensors
    slots = adapters * cap

    loads = [
        pltpu.make_async_copy(
            weight_hbm.at[pl.ds(i * chunk, chunk)], weight.at[pl.ds(i * chunk, chunk)], weight_sem.at[i]
        )
        for i in range(W_CHUNKS)
    ]
    for load in loads:
        load.start()
    load_down = pltpu.make_async_copy(down_hbm, down, down_sem)
    load_down.start()

    barrier = pltpu.get_barrier_semaphore()

    def greet_adapter(d, carry):
        pl.semaphore_signal(barrier, inc=1, device_id=(lax.rem(a + d, adapters), t), device_id_type=MESH)
        return carry

    lax.fori_loop(1, adapters, greet_adapter, 0)
    for d in range(1, tensors):
        pl.semaphore_signal(barrier, inc=1, device_id=(a, lax.rem(t + d, tensors)), device_id_type=MESH)

    core = lax.rem(t, 2)
    square = jnp.zeros((rows, 128), F32)
    for half_ref in (near_ref, far_ref):
        for i in range(2):
            part = half_ref[:, i * quarter:(i + 1) * quarter].astype(F32)
            part = part * part
            for j in range(quarter // 128):
                square = square + part[:, j * 128:(j + 1) * 128]
    inverse = lax.rsqrt(jnp.sum(square, axis=1, keepdims=True) / width + EPSILON)
    for half_ref, parity in ((near_ref, core), (far_ref, 1 - core)):
        for i in range(2):
            cols = pl.ds(pl.multiple_of((2 * i + parity) * quarter, quarter), quarter)
            normed[:, cols] = (
                half_ref[:, i * quarter:(i + 1) * quarter].astype(F32) * inverse * gain_ref[:, cols].astype(F32)
            ).astype(BF16)

    mine = normed[:, pl.ds(pl.multiple_of(t * quarter, quarter), quarter)]
    out_rows[:, :, :quarter] = jnp.dot(
        pick_ref[...], mine, preferred_element_type=F32
    ).astype(BF16).reshape(adapters, cap, quarter)
    out_rows[:, :, quarter:] = ids_ref[...].reshape(adapters, cap, 128)

    pl.semaphore_wait(barrier, adapters - 1 + tensors - 1)

    def row_copy(d):
        other = lax.rem(a + d, adapters)
        return pltpu.make_async_remote_copy(
            src_ref=out_rows.at[other], dst_ref=in_rows.at[a], send_sem=row_send.at[d],
            recv_sem=row_recv.at[adapters - d], device_id=(other, t), device_id_type=MESH,
        )

    def back_copy(d):
        other = lax.rem(a + d, adapters)
        return pltpu.make_async_remote_copy(
            src_ref=delta.at[other], dst_ref=back.at[a], send_sem=back_send.at[d],
            recv_sem=back_recv.at[adapters - d], device_id=(other, t), device_id_type=MESH,
        )

    def row_arrival(d):
        other = lax.rem(a + d, adapters)
        return pltpu.make_async_remote_copy(
            src_ref=out_rows.at[other], dst_ref=in_rows.at[other], send_sem=row_send.at[d],
            recv_sem=row_recv.at[d], device_id=(other, t), device_id_type=MESH,
        )

    def back_arrival(d):
        other = lax.rem(a + d, adapters)
        return pltpu.make_async_remote_copy(
            src_ref=delta.at[other], dst_ref=back.at[other], send_sem=back_send.at[d],
            recv_sem=back_recv.at[d], device_id=(other, t), device_id_type=MESH,
        )

    def each(function):
        def step(d, carry):
            function(d)
            return carry

        lax.fori_loop(1, adapters, step, 0)

    each(lambda d: row_copy(d).start())
    in_rows[a] = out_rows[a]

    for i in range(W_CHUNKS):
        loads[i].wait()
        part = jnp.dot(
            normed[:, i * chunk:(i + 1) * chunk], weight[i * chunk:(i + 1) * chunk, :], preferred_element_type=F32
        )
        base[...] = part if i == 0 else base[...] + part
    load_down.wait()

    each(lambda d: row_arrival(d).wait_recv())

    lane = lax.broadcasted_iota(jnp.int32, (slots, 128), 1)
    odd = jnp.where(lane >= ADAPTER_RANK, 1.0, 0.0)
    ids = in_rows[:, :, quarter:].reshape(slots, 128).astype(F32) - odd
    got = in_rows[:, :, :quarter].reshape(slots, quarter)
    low = jnp.zeros((slots, 128), F32)
    wide = 2
    for j in range(0, down.shape[1] // 128, wide):
        part = jnp.dot(got, down[:, j * 128:(j + wide) * 128], preferred_element_type=F32)
        for i in range(wide):
            low = low + jnp.where(ids == 2.0 * (j + i), part[:, i * 128:(i + 1) * 128], 0.0)
    low_out[...] = low.astype(BF16)

    shares = []
    for d in range(1, tensors):
        other = lax.rem(t + d, tensors)
        share = pltpu.make_async_remote_copy(
            src_ref=low_out, dst_ref=low_in.at[tensors - d], send_sem=low_send.at[d],
            recv_sem=low_recv.at[tensors - d], device_id=(a, other), device_id_type=MESH,
        )
        share.start()
        shares.append(share)
    for share in shares:
        share.wait()
    for d in range(1, tensors):
        low = low + low_in[d].astype(F32)
    low = low.astype(BF16).astype(F32)

    spread = jnp.concatenate(
        [jnp.where(ids == 2.0 * j, low, 0.0).astype(BF16) for j in range(down.shape[1] // 128)], axis=1
    )
    delta[...] = (
        ADAPTER_SCALE * jnp.dot(spread, up_ref[...], preferred_element_type=F32)
    ).astype(BF16).reshape(delta.shape)
    each(lambda d: back_copy(d).start())
    back[a] = delta[a]
    each(lambda d: back_arrival(d).wait_recv())

    update = jnp.dot(place_ref[...], back[...].reshape(slots, -1), preferred_element_type=F32)
    new_kv = (base[...] + update).astype(BF16)
    new_kv_ref[...] = new_kv

    kv_heads = new_kv.shape[1] // (2 * HEAD_SIZE)
    group = q_ref.shape[1] // HEAD_SIZE // kv_heads
    for k in range(kv_heads):
        key = new_kv[:, 2 * k * HEAD_SIZE:(2 * k + 1) * HEAD_SIZE].astype(F32)
        value = new_kv[:, (2 * k + 1) * HEAD_SIZE:(2 * k + 2) * HEAD_SIZE].astype(F32)
        for g in range(group):
            h = k * group + g
            cols = slice(h * HEAD_SIZE, (h + 1) * HEAD_SIZE)
            own = jnp.sum(q_ref[:, cols].astype(F32) * key, axis=1, keepdims=True) * SCALE
            cache_top = top_ref[:, h:h + 1]
            top = jnp.maximum(cache_top, own)
            shrink = jnp.exp(cache_top - top)
            weight_own = jnp.exp(own - top).astype(BF16).astype(F32)
            attn_ref[:, cols] = (
                (acc_ref[:, cols] * shrink + weight_own * value)
                / (total_ref[:, h:h + 1] * shrink + weight_own)
            ).astype(BF16)

    each(lambda d: row_copy(d).wait_send())
    each(lambda d: back_copy(d).wait_send())


def finish_rows(
    adapters, tensors, cap, near, far, gain, weight, down, up, pick, place, ids, queries, acc, top, total
):
    rows, width = near.shape[0], weight.shape[0]
    columns = weight.shape[1]
    slots = adapters * cap
    quarter = width // tensors
    vmem = pl.BlockSpec(memory_space=pltpu.VMEM)
    hbm = pl.BlockSpec(memory_space=pl.ANY)
    dma = pltpu.SemaphoreType.DMA
    return pl.pallas_call(
        functools.partial(rows_kernel, adapters, tensors, cap),
        out_shape=(
            jax.ShapeDtypeStruct((rows, columns), BF16),
            jax.ShapeDtypeStruct(queries.shape, BF16),
        ),
        in_specs=[vmem, vmem, vmem, hbm, hbm, vmem, vmem, vmem, vmem, vmem, vmem, vmem, vmem],
        out_specs=(vmem, vmem),
        scratch_shapes=[
            pltpu.VMEM(weight.shape, BF16),
            pltpu.VMEM(down.shape, BF16),
            pltpu.VMEM((rows, width), BF16),
            pltpu.VMEM((adapters, cap, quarter + 128), BF16),
            pltpu.VMEM((adapters, cap, quarter + 128), BF16),
            pltpu.VMEM((slots, 128), BF16),
            pltpu.VMEM((tensors, slots, 128), BF16),
            pltpu.VMEM((adapters, cap, columns), BF16),
            pltpu.VMEM((adapters, cap, columns), BF16),
            pltpu.VMEM((rows, columns), F32),
            dma((W_CHUNKS,)),
            dma,
            dma((adapters,)),
            dma((adapters,)),
            dma((tensors,)),
            dma((tensors,)),
            dma((adapters,)),
            dma((adapters,)),
        ],
        compiler_params=pltpu.CompilerParams(
            collective_id=0, has_side_effects=True, vmem_limit_bytes=59 * 2**20
        ),
        cost_estimate=pl.CostEstimate(
            flops=2 * rows * width * columns + 2 * slots * down.size, bytes_accessed=2 * (weight.size + down.size),
            transcendentals=0,
        ),
    )(near, far, gain, weight, down, up, pick, place, ids, queries, acc, top, total)


def per_device(
    partials,
    residual,
    attention_norm_gain,
    key_value_weight,
    adapter_down_weight,
    adapter_up_weight,
    row_adapter_index,
    queries,
    key_value_cache,
    prompt_cache_length,
):
    rows, width = residual.shape
    tensors = lax.axis_size("tensor")
    adapters = lax.axis_size("adapter")
    t = lax.axis_index("tensor")
    core = t % 2
    swap_core = [(i, i ^ 1) for i in range(tensors)]
    swap_chip = [(i, i ^ 2) for i in range(tensors)]

    cap = max(16, 4 * rows // adapters)
    held = adapter_down_weight.shape[1] // ADAPTER_RANK
    order = jnp.arange(rows)
    earlier = order[None, :] < order[:, None]
    own_owner = row_adapter_index // held
    own_rank = jnp.sum(((own_owner[:, None] == own_owner[None, :]) & earlier).astype(jnp.int32), axis=1)
    row_slot = own_owner * cap + own_rank
    slots = jnp.arange(adapters * cap)
    pick = (slots[:, None] == row_slot[None, :]).astype(BF16)
    local = (row_adapter_index % held)[None, :] + 1
    ids = jnp.sum(jnp.where(slots[:, None] == row_slot[None, :], local, 0), axis=1) - 1
    ids = jnp.broadcast_to(ids[:, None], (adapters * cap, 128)).astype(BF16)
    place = (row_slot[:, None] == slots[None, :]).astype(BF16)

    quarter = width // tensors

    def quarters(array, parity):
        return jnp.concatenate(
            [lax.dynamic_slice_in_dim(array, (2 * i + parity) * quarter, quarter, 1) for i in range(2)], axis=1
        )

    taken = lax.ppermute(quarters(partials[0], 1 - core), "tensor", swap_core)
    chip_sum = (quarters(partials[0], core).astype(F32) + taken.astype(F32)).astype(BF16)
    other_sum = lax.ppermute(chip_sum, "tensor", swap_chip)
    flat_weight = key_value_weight.reshape(width, -1)
    flat_up = adapter_up_weight.reshape(adapter_up_weight.shape[0], -1)
    acc, top, total = attend_cache(queries, key_value_cache, prompt_cache_length)
    other_sum, acc, top, total, flat_weight, flat_up, pick, place, ids = lax.optimization_barrier(
        (other_sum, acc, top, total, flat_weight, flat_up, pick, place, ids)
    )
    near = (
        quarters(residual, core).astype(F32) + (chip_sum.astype(F32) + other_sum.astype(F32))
    ).astype(BF16)
    far = lax.ppermute(near, "tensor", swap_core)
    hidden_part = lax.dynamic_slice_in_dim(near, (t // 2) * quarter, quarter, 1)

    new_kv, attended = finish_rows(
        adapters, tensors, cap, near, far, attention_norm_gain[None, :],
        flat_weight, adapter_down_weight, flat_up, pick, place, ids, queries, acc, top, total,
    )
    return hidden_part, new_kv.reshape(rows, key_value_weight.shape[1], 2 * HEAD_SIZE), attended


def solution(mesh):
    return jax.shard_map(
        per_device,
        mesh=mesh,
        in_specs=(
            P("tensor", "adapter", None),
            P("adapter", None),
            P(),
            P(None, "tensor", None),
            P("tensor", "adapter"),
            P("adapter", "tensor", None),
            P("adapter"),
            P("adapter", "tensor"),
            P("adapter", None, None, "tensor"),
            P("adapter"),
        ),
        out_specs=(P("adapter", "tensor"), P("adapter", "tensor", None), P("adapter", "tensor")),
        check_vma=False,
    )
```

```python
import functools

import jax
import jax.numpy as jnp
from jax import lax
from jax.experimental import pallas as pl
from jax.experimental.pallas import tpu as pltpu
from jax.sharding import PartitionSpec as P

HEAD_SIZE = 128
ADAPTER_RANK = 64
FAN = 8
EPSILON = 1e-05
ADAPTER_SCALE = 0.5
MESH = pl.DeviceIdType.MESH
F32 = jnp.float32
BF16 = jnp.bfloat16
SCALE = HEAD_SIZE ** (-0.5)


def attend_cache(q_ref, cache, length_ref, loads, acc_ref, top_ref, total_ref):
    prompts, _, slots, width = cache.shape
    kv_heads = width // HEAD_SIZE
    group = q_ref.shape[1] // HEAD_SIZE // kv_heads
    lane = lax.broadcasted_iota(jnp.int32, (FAN, 128), 1)

    def pair(i, carry):
        base = pl.multiple_of(i * 2 * FAN, 2 * FAN)
        loads(i).wait()
        both = q_ref[pl.ds(base, 2 * FAN), :].astype(F32)
        for n in range(2):
            q = both[n * FAN:(n + 1) * FAN]
            length = length_ref[2 * i + n][:1, :1]
            tops = jnp.zeros((FAN, 128), F32)
            totals = jnp.zeros((FAN, 128), F32)
            out_rows = pl.ds(pl.multiple_of(base + n * FAN, FAN), FAN)
            for k in range(kv_heads):
                cols = slice(k * HEAD_SIZE, (k + 1) * HEAD_SIZE)
                stack = jnp.concatenate(
                    [q[:, (k * group + g) * HEAD_SIZE:(k * group + g + 1) * HEAD_SIZE] for g in range(group)], axis=0
                ).astype(BF16)
                scores = lax.dot_general(
                    stack, cache[2 * i + n, 0, :, cols], (((1,), (1,)), ((), ())), preferred_element_type=F32
                ) * SCALE
                slot = lax.broadcasted_iota(jnp.int32, scores.shape, 1)
                scores = jnp.where(slot < length, scores, -jnp.inf)
                top = jnp.max(scores, axis=1, keepdims=True)
                weights = jnp.exp(scores - top).astype(BF16)
                total = jnp.sum(weights.astype(F32), axis=1, keepdims=True)
                acc = jnp.dot(weights, cache[2 * i + n, 1, :, cols], preferred_element_type=F32)
                for g in range(group):
                    h = k * group + g
                    rows = slice(g * FAN, (g + 1) * FAN)
                    acc_ref[out_rows, h * HEAD_SIZE:(h + 1) * HEAD_SIZE] = acc[rows]
                    tops = jnp.where(lane == h, top[rows], tops)
                    totals = jnp.where(lane == h, total[rows], totals)
            top_ref[out_rows, :] = tops
            total_ref[out_rows, :] = totals
        return carry

    lax.fori_loop(0, prompts // 2, pair, 0)


W_CHUNKS = 4


def rows_kernel(
    adapters, tensors, cap,
    near_ref, gain_ref, weight_hbm, down_hbm, cache_hbm, up_ref, pick_ref, place_ref, ids_ref,
    q_ref, length_ref,
    new_kv_ref, attn_ref,
    weight, down, cache, acc_ref, top_ref, total_ref, far_ref, square_out, square_in,
    normed, out_rows, in_rows, low_out, low_in, delta, back, base,
    weight_sem, down_sem, cache_sem, far_sem, square_sem,
    row_send, row_recv, low_send, low_recv, back_send, back_recv,
):
    a = lax.axis_index("adapter")
    t = lax.axis_index("tensor")
    rows, width = near_ref.shape[0], weight_hbm.shape[0]
    chunk = width // W_CHUNKS
    quarter = width // tensors
    slots = adapters * cap

    loads = [
        pltpu.make_async_copy(
            weight_hbm.at[pl.ds(i * chunk, chunk)], weight.at[pl.ds(i * chunk, chunk)], weight_sem.at[i]
        )
        for i in range(W_CHUNKS)
    ]
    for load in loads:
        load.start()
    load_down = pltpu.make_async_copy(down_hbm, down, down_sem)
    load_down.start()

    def load_cache(i):
        return pltpu.make_async_copy(
            cache_hbm.at[pl.ds(2 * i, 2)], cache.at[pl.ds(2 * i, 2)], cache_sem.at[i]
        )

    for i in range(cache.shape[0] // 2):
        load_cache(i).start()

    barrier = pltpu.get_barrier_semaphore()

    def greet_adapter(d, carry):
        pl.semaphore_signal(barrier, inc=1, device_id=(lax.rem(a + d, adapters), t), device_id_type=MESH)
        return carry

    lax.fori_loop(1, adapters, greet_adapter, 0)
    for d in range(1, tensors):
        pl.semaphore_signal(barrier, inc=1, device_id=(a, lax.rem(t + d, tensors)), device_id_type=MESH)

    core = lax.rem(t, 2)
    square = jnp.zeros((rows, 128), F32)
    for i in range(2):
        part = near_ref[:, i * quarter:(i + 1) * quarter].astype(F32)
        part = part * part
        for j in range(quarter // 128):
            square = square + part[:, j * 128:(j + 1) * 128]
    square_out[...] = square

    pl.semaphore_wait(barrier, adapters - 1 + tensors - 1)
    beside = t + 1 - 2 * core
    send_square = pltpu.make_async_remote_copy(
        src_ref=square_out, dst_ref=square_in, send_sem=square_sem.at[0], recv_sem=square_sem.at[1],
        device_id=(a, beside), device_id_type=MESH,
    )
    send_square.start()
    send_half = pltpu.make_async_remote_copy(
        src_ref=near_ref, dst_ref=far_ref, send_sem=far_sem.at[0], recv_sem=far_sem.at[1],
        device_id=(a, beside), device_id_type=MESH,
    )
    send_half.start()
    send_square.wait()
    both = square + square_in[...]
    inverse = lax.rsqrt(jnp.sum(both, axis=1, keepdims=True) / width + EPSILON)

    def normalize(half_ref, parity):
        for i in range(2):
            cols = pl.ds(pl.multiple_of((2 * i + parity) * quarter, quarter), quarter)
            normed[:, cols] = (
                half_ref[:, i * quarter:(i + 1) * quarter].astype(F32) * inverse * gain_ref[:, cols].astype(F32)
            ).astype(BF16)

    normalize(near_ref, core)
    mine = normed[:, pl.ds(pl.multiple_of(t * quarter, quarter), quarter)]
    out_rows[:, :, :quarter] = jnp.dot(
        pick_ref[...], mine, preferred_element_type=F32
    ).astype(BF16).reshape(adapters, cap, quarter)
    out_rows[:, :, quarter:] = ids_ref[...].reshape(adapters, cap, 128)


    def row_copy(d):
        other = lax.rem(a + d, adapters)
        return pltpu.make_async_remote_copy(
            src_ref=out_rows.at[other], dst_ref=in_rows.at[a], send_sem=row_send.at[d],
            recv_sem=row_recv.at[adapters - d], device_id=(other, t), device_id_type=MESH,
        )

    def back_copy(d):
        other = lax.rem(a + d, adapters)
        return pltpu.make_async_remote_copy(
            src_ref=delta.at[other], dst_ref=back.at[a], send_sem=back_send.at[d],
            recv_sem=back_recv.at[adapters - d], device_id=(other, t), device_id_type=MESH,
        )

    def row_arrival(d):
        other = lax.rem(a + d, adapters)
        return pltpu.make_async_remote_copy(
            src_ref=out_rows.at[other], dst_ref=in_rows.at[other], send_sem=row_send.at[d],
            recv_sem=row_recv.at[d], device_id=(other, t), device_id_type=MESH,
        )

    def back_arrival(d):
        other = lax.rem(a + d, adapters)
        return pltpu.make_async_remote_copy(
            src_ref=delta.at[other], dst_ref=back.at[other], send_sem=back_send.at[d],
            recv_sem=back_recv.at[d], device_id=(other, t), device_id_type=MESH,
        )

    def each(function):
        def step(d, carry):
            function(d)
            return carry

        lax.fori_loop(1, adapters, step, 0)

    each(lambda d: row_copy(d).start())
    in_rows[a] = out_rows[a]

    attend_cache(q_ref, cache, length_ref, load_cache, acc_ref, top_ref, total_ref)
    send_half.wait()
    normalize(far_ref, 1 - core)
    for i in range(W_CHUNKS):
        loads[i].wait()
        part = jnp.dot(
            normed[:, i * chunk:(i + 1) * chunk], weight[i * chunk:(i + 1) * chunk, :], preferred_element_type=F32
        )
        base[...] = part if i == 0 else base[...] + part
    load_down.wait()

    each(lambda d: row_arrival(d).wait_recv())

    lane = lax.broadcasted_iota(jnp.int32, (slots, 128), 1)
    odd = jnp.where(lane >= ADAPTER_RANK, 1.0, 0.0)
    ids = in_rows[:, :, quarter:].reshape(slots, 128).astype(F32) - odd
    got = in_rows[:, :, :quarter].reshape(slots, quarter)
    low = jnp.zeros((slots, 128), F32)
    wide = 2
    for j in range(0, down.shape[1] // 128, wide):
        part = jnp.dot(got, down[:, j * 128:(j + wide) * 128], preferred_element_type=F32)
        for i in range(wide):
            low = low + jnp.where(ids == 2.0 * (j + i), part[:, i * 128:(i + 1) * 128], 0.0)
    low_out[...] = low.astype(BF16)

    shares = []
    for d in range(1, tensors):
        other = lax.rem(t + d, tensors)
        share = pltpu.make_async_remote_copy(
            src_ref=low_out, dst_ref=low_in.at[tensors - d], send_sem=low_send.at[d],
            recv_sem=low_recv.at[tensors - d], device_id=(a, other), device_id_type=MESH,
        )
        share.start()
        shares.append(share)
    for share in shares:
        share.wait()
    for d in range(1, tensors):
        low = low + low_in[d].astype(F32)
    low = low.astype(BF16).astype(F32)

    spread = jnp.concatenate(
        [jnp.where(ids == 2.0 * j, low, 0.0).astype(BF16) for j in range(down.shape[1] // 128)], axis=1
    )
    delta[...] = (
        ADAPTER_SCALE * jnp.dot(spread, up_ref[...], preferred_element_type=F32)
    ).astype(BF16).reshape(delta.shape)
    each(lambda d: back_copy(d).start())
    back[a] = delta[a]
    each(lambda d: back_arrival(d).wait_recv())

    update = jnp.dot(place_ref[...], back[...].reshape(slots, -1), preferred_element_type=F32)
    new_kv = (base[...] + update).astype(BF16)
    new_kv_ref[...] = new_kv

    kv_heads = new_kv.shape[1] // (2 * HEAD_SIZE)
    group = q_ref.shape[1] // HEAD_SIZE // kv_heads
    for k in range(kv_heads):
        key = new_kv[:, 2 * k * HEAD_SIZE:(2 * k + 1) * HEAD_SIZE].astype(F32)
        value = new_kv[:, (2 * k + 1) * HEAD_SIZE:(2 * k + 2) * HEAD_SIZE].astype(F32)
        for g in range(group):
            h = k * group + g
            cols = slice(h * HEAD_SIZE, (h + 1) * HEAD_SIZE)
            own = jnp.sum(q_ref[:, cols].astype(F32) * key, axis=1, keepdims=True) * SCALE
            cache_top = top_ref[:, h:h + 1]
            top = jnp.maximum(cache_top, own)
            shrink = jnp.exp(cache_top - top)
            weight_own = jnp.exp(own - top).astype(BF16).astype(F32)
            attn_ref[:, cols] = (
                (acc_ref[:, cols] * shrink + weight_own * value)
                / (total_ref[:, h:h + 1] * shrink + weight_own)
            ).astype(BF16)

    each(lambda d: row_copy(d).wait_send())
    each(lambda d: back_copy(d).wait_send())


def finish_rows(
    adapters, tensors, cap, near, gain, weight, down, cache, up, pick, place, ids, queries, lengths
):
    rows, width = near.shape[0], weight.shape[0]
    columns = weight.shape[1]
    slots = adapters * cap
    quarter = width // tensors
    vmem = pl.BlockSpec(memory_space=pltpu.VMEM)
    hbm = pl.BlockSpec(memory_space=pl.ANY)
    dma = pltpu.SemaphoreType.DMA
    return pl.pallas_call(
        functools.partial(rows_kernel, adapters, tensors, cap),
        out_shape=(
            jax.ShapeDtypeStruct((rows, columns), BF16),
            jax.ShapeDtypeStruct(queries.shape, BF16),
        ),
        in_specs=[vmem, vmem, hbm, hbm, hbm, vmem, vmem, vmem, vmem, vmem, vmem],
        out_specs=(vmem, vmem),
        scratch_shapes=[
            pltpu.VMEM(weight.shape, BF16),
            pltpu.VMEM(down.shape, BF16),
            pltpu.VMEM(cache.shape, BF16),
            pltpu.VMEM(queries.shape, F32),
            pltpu.VMEM((rows, 128), F32),
            pltpu.VMEM((rows, 128), F32),
            pltpu.VMEM(near.shape, BF16),
            pltpu.VMEM((rows, 128), F32),
            pltpu.VMEM((rows, 128), F32),
            pltpu.VMEM((rows, width), BF16),
            pltpu.VMEM((adapters, cap, quarter + 128), BF16),
            pltpu.VMEM((adapters, cap, quarter + 128), BF16),
            pltpu.VMEM((slots, 128), BF16),
            pltpu.VMEM((tensors, slots, 128), BF16),
            pltpu.VMEM((adapters, cap, columns), BF16),
            pltpu.VMEM((adapters, cap, columns), BF16),
            pltpu.VMEM((rows, columns), F32),
            dma((W_CHUNKS,)),
            dma,
            dma((cache.shape[0] // 2,)),
            dma((2,)),
            dma((2,)),
            dma((adapters,)),
            dma((adapters,)),
            dma((tensors,)),
            dma((tensors,)),
            dma((adapters,)),
            dma((adapters,)),
        ],
        compiler_params=pltpu.CompilerParams(
            collective_id=0, has_side_effects=True, vmem_limit_bytes=50 * 2**20
        ),
        cost_estimate=pl.CostEstimate(
            flops=2 * rows * width * columns + 2 * slots * down.size, bytes_accessed=2 * (weight.size + down.size),
            transcendentals=0,
        ),
    )(near, gain, weight, down, cache, up, pick, place, ids, queries, lengths)


def per_device(
    partials,
    residual,
    attention_norm_gain,
    key_value_weight,
    adapter_down_weight,
    adapter_up_weight,
    row_adapter_index,
    queries,
    key_value_cache,
    prompt_cache_length,
):
    rows, width = residual.shape
    tensors = lax.axis_size("tensor")
    adapters = lax.axis_size("adapter")
    t = lax.axis_index("tensor")
    core = t % 2
    swap_core = [(i, i ^ 1) for i in range(tensors)]
    swap_chip = [(i, i ^ 2) for i in range(tensors)]

    cap = max(16, 4 * rows // adapters)
    held = adapter_down_weight.shape[1] // ADAPTER_RANK
    order = jnp.arange(rows)
    earlier = order[None, :] < order[:, None]
    own_owner = row_adapter_index // held
    own_rank = jnp.sum(((own_owner[:, None] == own_owner[None, :]) & earlier).astype(jnp.int32), axis=1)
    row_slot = own_owner * cap + own_rank
    slots = jnp.arange(adapters * cap)
    pick = (slots[:, None] == row_slot[None, :]).astype(BF16)
    local = (row_adapter_index % held)[None, :] + 1
    ids = jnp.sum(jnp.where(slots[:, None] == row_slot[None, :], local, 0), axis=1) - 1
    ids = jnp.broadcast_to(ids[:, None], (adapters * cap, 128)).astype(BF16)
    place = (row_slot[:, None] == slots[None, :]).astype(BF16)

    quarter = width // tensors

    def quarters(array, parity):
        return jnp.concatenate(
            [lax.dynamic_slice_in_dim(array, (2 * i + parity) * quarter, quarter, 1) for i in range(2)], axis=1
        )

    gain = attention_norm_gain[None, :]
    lengths = jnp.broadcast_to(prompt_cache_length[:, None, None], (prompt_cache_length.shape[0], 8, 128))
    taken = lax.ppermute(quarters(partials[0], 1 - core), "tensor", swap_core)
    taken, pick, place, ids, gain, lengths = lax.optimization_barrier((taken, pick, place, ids, gain, lengths))
    chip_sum = (quarters(partials[0], core).astype(F32) + taken.astype(F32)).astype(BF16)
    other_sum = lax.ppermute(chip_sum, "tensor", swap_chip)
    flat_weight = key_value_weight.reshape(width, -1)
    flat_up = adapter_up_weight.reshape(adapter_up_weight.shape[0], -1)
    other_sum, flat_weight, flat_up = lax.optimization_barrier((other_sum, flat_weight, flat_up))
    near = (
        quarters(residual, core).astype(F32) + (chip_sum.astype(F32) + other_sum.astype(F32))
    ).astype(BF16)
    hidden_part = lax.dynamic_slice_in_dim(near, (t // 2) * quarter, quarter, 1)
    new_kv, attended = finish_rows(
        adapters, tensors, cap, near, gain, flat_weight, adapter_down_weight, key_value_cache, flat_up,
        pick, place, ids, queries, lengths,
    )
    return hidden_part, new_kv.reshape(rows, key_value_weight.shape[1], 2 * HEAD_SIZE), attended


def solution(mesh):
    return jax.shard_map(
        per_device,
        mesh=mesh,
        in_specs=(
            P("tensor", "adapter", None),
            P("adapter", None),
            P(),
            P(None, "tensor", None),
            P("tensor", "adapter"),
            P("adapter", "tensor", None),
            P("adapter"),
            P("adapter", "tensor"),
            P("adapter", None, None, "tensor"),
            P("adapter"),
        ),
        out_specs=(P("adapter", "tensor"), P("adapter", "tensor", None), P("adapter", "tensor")),
        check_vma=False,
    )
```

```python
import functools

import jax
import jax.numpy as jnp
from jax import lax
from jax.experimental import pallas as pl
from jax.experimental.pallas import tpu as pltpu
from jax.sharding import PartitionSpec as P

HEAD_SIZE = 128
ADAPTER_RANK = 64
FAN = 8
EPSILON = 1e-05
ADAPTER_SCALE = 0.5
MESH = pl.DeviceIdType.MESH
F32 = jnp.float32
BF16 = jnp.bfloat16
SCALE = HEAD_SIZE ** (-0.5)


def attend_cache(q_ref, cache, length_ref, loads, acc_ref, top_ref, total_ref):
    prompts, _, slots, width = cache.shape
    kv_heads = width // HEAD_SIZE
    group = q_ref.shape[1] // HEAD_SIZE // kv_heads
    lane = lax.broadcasted_iota(jnp.int32, (FAN, 128), 1)

    def pair(i, carry):
        base = pl.multiple_of(i * 2 * FAN, 2 * FAN)
        loads(i).wait()
        both = q_ref[pl.ds(base, 2 * FAN), :].astype(F32)
        for n in range(2):
            q = both[n * FAN:(n + 1) * FAN]
            length = length_ref[2 * i + n][:1, :1]
            tops = jnp.zeros((FAN, 128), F32)
            totals = jnp.zeros((FAN, 128), F32)
            out_rows = pl.ds(pl.multiple_of(base + n * FAN, FAN), FAN)
            for k in range(kv_heads):
                cols = slice(k * HEAD_SIZE, (k + 1) * HEAD_SIZE)
                stack = jnp.concatenate(
                    [q[:, (k * group + g) * HEAD_SIZE:(k * group + g + 1) * HEAD_SIZE] for g in range(group)], axis=0
                ).astype(BF16)
                scores = lax.dot_general(
                    stack, cache[2 * i + n, 0, :, cols], (((1,), (1,)), ((), ())), preferred_element_type=F32
                ) * SCALE
                slot = lax.broadcasted_iota(jnp.int32, scores.shape, 1)
                scores = jnp.where(slot < length, scores, -jnp.inf)
                top = jnp.max(scores, axis=1, keepdims=True)
                weights = jnp.exp(scores - top).astype(BF16)
                total = jnp.sum(weights.astype(F32), axis=1, keepdims=True)
                acc = jnp.dot(weights, cache[2 * i + n, 1, :, cols], preferred_element_type=F32)
                for g in range(group):
                    h = k * group + g
                    rows = slice(g * FAN, (g + 1) * FAN)
                    acc_ref[out_rows, h * HEAD_SIZE:(h + 1) * HEAD_SIZE] = acc[rows]
                    tops = jnp.where(lane == h, top[rows], tops)
                    totals = jnp.where(lane == h, total[rows], totals)
            top_ref[out_rows, :] = tops
            total_ref[out_rows, :] = totals
        return carry

    lax.fori_loop(0, prompts // 2, pair, 0)


W_CHUNKS = 4


def rows_kernel(
    adapters, tensors, cap,
    near_ref, gain_ref, weight_hbm, down_hbm, cache_hbm, up_ref, pick_ref, place_ref, ids_ref,
    q_ref, length_ref,
    new_kv_ref, attn_ref,
    weight, down, cache, acc_ref, top_ref, total_ref, far_ref, square_out, square_in,
    normed, out_rows, in_rows, low_own, low_out, low_in, delta, back, base,
    weight_sem, down_sem, cache_sem, far_sem, square_sem,
    row_send, row_recv, low_send, low_recv, back_send, back_recv,
):
    a = lax.axis_index("adapter")
    t = lax.axis_index("tensor")
    rows, width = near_ref.shape[0], weight_hbm.shape[0]
    chunk = width // W_CHUNKS
    quarter = width // tensors
    slots = adapters * cap

    loads = [
        pltpu.make_async_copy(
            weight_hbm.at[pl.ds(i * chunk, chunk)], weight.at[pl.ds(i * chunk, chunk)], weight_sem.at[i]
        )
        for i in range(W_CHUNKS)
    ]
    for load in loads:
        load.start()
    load_down = pltpu.make_async_copy(down_hbm, down, down_sem)
    load_down.start()

    def load_cache(i):
        return pltpu.make_async_copy(
            cache_hbm.at[pl.ds(2 * i, 2)], cache.at[pl.ds(2 * i, 2)], cache_sem.at[i]
        )

    for i in range(cache.shape[0] // 2):
        load_cache(i).start()

    barrier = pltpu.get_barrier_semaphore()

    def greet_adapter(d, carry):
        pl.semaphore_signal(barrier, inc=1, device_id=(lax.rem(a + d, adapters), t), device_id_type=MESH)
        return carry

    lax.fori_loop(1, adapters, greet_adapter, 0)
    for d in range(1, tensors):
        pl.semaphore_signal(barrier, inc=1, device_id=(a, lax.rem(t + d, tensors)), device_id_type=MESH)

    core = lax.rem(t, 2)
    square = jnp.zeros((rows, 128), F32)
    for i in range(2):
        part = near_ref[:, i * quarter:(i + 1) * quarter].astype(F32)
        part = part * part
        for j in range(quarter // 128):
            square = square + part[:, j * 128:(j + 1) * 128]
    square_out[...] = square

    pl.semaphore_wait(barrier, adapters - 1 + tensors - 1)
    beside = t + 1 - 2 * core
    send_square = pltpu.make_async_remote_copy(
        src_ref=square_out, dst_ref=square_in, send_sem=square_sem.at[0], recv_sem=square_sem.at[1],
        device_id=(a, beside), device_id_type=MESH,
    )
    send_square.start()
    send_half = pltpu.make_async_remote_copy(
        src_ref=near_ref, dst_ref=far_ref, send_sem=far_sem.at[0], recv_sem=far_sem.at[1],
        device_id=(a, beside), device_id_type=MESH,
    )
    send_half.start()
    send_square.wait()
    both = square + square_in[...]
    inverse = lax.rsqrt(jnp.sum(both, axis=1, keepdims=True) / width + EPSILON)

    def normalize(half_ref, parity):
        for i in range(2):
            cols = pl.ds(pl.multiple_of((2 * i + parity) * quarter, quarter), quarter)
            normed[:, cols] = (
                half_ref[:, i * quarter:(i + 1) * quarter].astype(F32) * inverse * gain_ref[:, cols].astype(F32)
            ).astype(BF16)

    normalize(near_ref, core)
    mine = normed[:, pl.ds(pl.multiple_of(t * quarter, quarter), quarter)]
    out_rows[:, :, :quarter] = jnp.dot(
        pick_ref[...], mine, preferred_element_type=F32
    ).astype(BF16).reshape(adapters, cap, quarter)
    out_rows[:, :, quarter:] = ids_ref[...].reshape(adapters, cap, 128)


    def row_copy(d):
        other = lax.rem(a + d, adapters)
        return pltpu.make_async_remote_copy(
            src_ref=out_rows.at[other], dst_ref=in_rows.at[a], send_sem=row_send.at[d],
            recv_sem=row_recv.at[adapters - d], device_id=(other, t), device_id_type=MESH,
        )

    def back_copy(d):
        other = lax.rem(a + d, adapters)
        return pltpu.make_async_remote_copy(
            src_ref=delta.at[other], dst_ref=back.at[a], send_sem=back_send.at[d],
            recv_sem=back_recv.at[adapters - d], device_id=(other, t), device_id_type=MESH,
        )

    def row_arrival(d):
        other = lax.rem(a + d, adapters)
        return pltpu.make_async_remote_copy(
            src_ref=out_rows.at[other], dst_ref=in_rows.at[other], send_sem=row_send.at[d],
            recv_sem=row_recv.at[d], device_id=(other, t), device_id_type=MESH,
        )

    def back_arrival(d):
        other = lax.rem(a + d, adapters)
        return pltpu.make_async_remote_copy(
            src_ref=delta.at[other], dst_ref=back.at[other], send_sem=back_send.at[d],
            recv_sem=back_recv.at[d], device_id=(other, t), device_id_type=MESH,
        )

    def each(function):
        def step(d, carry):
            function(d)
            return carry

        lax.fori_loop(1, adapters, step, 0)

    each(lambda d: row_copy(d).start())
    in_rows[a] = out_rows[a]

    attend_cache(q_ref, cache, length_ref, load_cache, acc_ref, top_ref, total_ref)
    send_half.wait()
    normalize(far_ref, 1 - core)
    for i in range(W_CHUNKS):
        loads[i].wait()
        part = jnp.dot(
            normed[:, i * chunk:(i + 1) * chunk], weight[i * chunk:(i + 1) * chunk, :], preferred_element_type=F32
        )
        base[...] = part if i == 0 else base[...] + part
    load_down.wait()

    side = adapters // 2
    for far in range(2):
        first = lax.rem(a // side + far, 2) * side

        def arrive(i, carry):
            d = lax.rem(first + i - a + adapters, adapters)

            @pl.when(d > 0)
            def _():
                row_arrival(d).wait_recv()

            return carry

        lax.fori_loop(0, side, arrive, 0)
        some = slots // 2
        odd = jnp.where(lax.broadcasted_iota(jnp.int32, (some, 128), 1) >= ADAPTER_RANK, 1.0, 0.0)
        block = in_rows[pl.ds(first, side)]
        ids = block[:, :, quarter:].reshape(some, 128).astype(F32) - odd
        got = block[:, :, :quarter].reshape(some, quarter)
        low = jnp.zeros((some, 128), F32)
        wide = 2
        for j in range(0, down.shape[1] // 128, wide):
            part = jnp.dot(got, down[:, j * 128:(j + wide) * 128], preferred_element_type=F32)
            for i in range(wide):
                low = low + jnp.where(ids == 2.0 * (j + i), part[:, i * 128:(i + 1) * 128], 0.0)
        low_own[pl.ds(pl.multiple_of(first * cap, some), some), :] = low
    low = low_own[...]
    odd = jnp.where(lax.broadcasted_iota(jnp.int32, (slots, 128), 1) >= ADAPTER_RANK, 1.0, 0.0)
    ids = in_rows[:, :, quarter:].reshape(slots, 128).astype(F32) - odd
    low_out[...] = low.astype(BF16)

    shares = []
    for d in range(1, tensors):
        other = lax.rem(t + d, tensors)
        share = pltpu.make_async_remote_copy(
            src_ref=low_out, dst_ref=low_in.at[tensors - d], send_sem=low_send.at[d],
            recv_sem=low_recv.at[tensors - d], device_id=(a, other), device_id_type=MESH,
        )
        share.start()
        shares.append(share)
    for share in shares:
        share.wait()
    for d in range(1, tensors):
        low = low + low_in[d].astype(F32)
    low = low.astype(BF16).astype(F32)

    spread = jnp.concatenate(
        [jnp.where(ids == 2.0 * j, low, 0.0).astype(BF16) for j in range(down.shape[1] // 128)], axis=1
    )
    delta[...] = (
        ADAPTER_SCALE * jnp.dot(spread, up_ref[...], preferred_element_type=F32)
    ).astype(BF16).reshape(delta.shape)
    each(lambda d: back_copy(d).start())
    back[a] = delta[a]
    each(lambda d: back_arrival(d).wait_recv())

    update = jnp.dot(place_ref[...], back[...].reshape(slots, -1), preferred_element_type=F32)
    new_kv = (base[...] + update).astype(BF16)
    new_kv_ref[...] = new_kv

    kv_heads = new_kv.shape[1] // (2 * HEAD_SIZE)
    group = q_ref.shape[1] // HEAD_SIZE // kv_heads
    for k in range(kv_heads):
        key = new_kv[:, 2 * k * HEAD_SIZE:(2 * k + 1) * HEAD_SIZE].astype(F32)
        value = new_kv[:, (2 * k + 1) * HEAD_SIZE:(2 * k + 2) * HEAD_SIZE].astype(F32)
        for g in range(group):
            h = k * group + g
            cols = slice(h * HEAD_SIZE, (h + 1) * HEAD_SIZE)
            own = jnp.sum(q_ref[:, cols].astype(F32) * key, axis=1, keepdims=True) * SCALE
            cache_top = top_ref[:, h:h + 1]
            top = jnp.maximum(cache_top, own)
            shrink = jnp.exp(cache_top - top)
            weight_own = jnp.exp(own - top).astype(BF16).astype(F32)
            attn_ref[:, cols] = (
                (acc_ref[:, cols] * shrink + weight_own * value)
                / (total_ref[:, h:h + 1] * shrink + weight_own)
            ).astype(BF16)

    each(lambda d: row_copy(d).wait_send())
    each(lambda d: back_copy(d).wait_send())


def finish_rows(
    adapters, tensors, cap, near, gain, weight, down, cache, up, pick, place, ids, queries, lengths
):
    rows, width = near.shape[0], weight.shape[0]
    columns = weight.shape[1]
    slots = adapters * cap
    quarter = width // tensors
    vmem = pl.BlockSpec(memory_space=pltpu.VMEM)
    hbm = pl.BlockSpec(memory_space=pl.ANY)
    dma = pltpu.SemaphoreType.DMA
    return pl.pallas_call(
        functools.partial(rows_kernel, adapters, tensors, cap),
        out_shape=(
            jax.ShapeDtypeStruct((rows, columns), BF16),
            jax.ShapeDtypeStruct(queries.shape, BF16),
        ),
        in_specs=[vmem, vmem, hbm, hbm, hbm, vmem, vmem, vmem, vmem, vmem, vmem],
        out_specs=(vmem, vmem),
        scratch_shapes=[
            pltpu.VMEM(weight.shape, BF16),
            pltpu.VMEM(down.shape, BF16),
            pltpu.VMEM(cache.shape, BF16),
            pltpu.VMEM(queries.shape, F32),
            pltpu.VMEM((rows, 128), F32),
            pltpu.VMEM((rows, 128), F32),
            pltpu.VMEM(near.shape, BF16),
            pltpu.VMEM((rows, 128), F32),
            pltpu.VMEM((rows, 128), F32),
            pltpu.VMEM((rows, width), BF16),
            pltpu.VMEM((adapters, cap, quarter + 128), BF16),
            pltpu.VMEM((adapters, cap, quarter + 128), BF16),
            pltpu.VMEM((slots, 128), F32),
            pltpu.VMEM((slots, 128), BF16),
            pltpu.VMEM((tensors, slots, 128), BF16),
            pltpu.VMEM((adapters, cap, columns), BF16),
            pltpu.VMEM((adapters, cap, columns), BF16),
            pltpu.VMEM((rows, columns), F32),
            dma((W_CHUNKS,)),
            dma,
            dma((cache.shape[0] // 2,)),
            dma((2,)),
            dma((2,)),
            dma((adapters,)),
            dma((adapters,)),
            dma((tensors,)),
            dma((tensors,)),
            dma((adapters,)),
            dma((adapters,)),
        ],
        compiler_params=pltpu.CompilerParams(
            collective_id=0, has_side_effects=True, vmem_limit_bytes=50 * 2**20
        ),
        cost_estimate=pl.CostEstimate(
            flops=2 * rows * width * columns + 2 * slots * down.size, bytes_accessed=2 * (weight.size + down.size),
            transcendentals=0,
        ),
    )(near, gain, weight, down, cache, up, pick, place, ids, queries, lengths)


def per_device(
    partials,
    residual,
    attention_norm_gain,
    key_value_weight,
    adapter_down_weight,
    adapter_up_weight,
    row_adapter_index,
    queries,
    key_value_cache,
    prompt_cache_length,
):
    rows, width = residual.shape
    tensors = lax.axis_size("tensor")
    adapters = lax.axis_size("adapter")
    t = lax.axis_index("tensor")
    core = t % 2
    swap_core = [(i, i ^ 1) for i in range(tensors)]
    swap_chip = [(i, i ^ 2) for i in range(tensors)]

    cap = max(16, 4 * rows // adapters)
    held = adapter_down_weight.shape[1] // ADAPTER_RANK
    order = jnp.arange(rows)
    earlier = order[None, :] < order[:, None]
    own_owner = row_adapter_index // held
    own_rank = jnp.sum(((own_owner[:, None] == own_owner[None, :]) & earlier).astype(jnp.int32), axis=1)
    row_slot = own_owner * cap + own_rank
    slots = jnp.arange(adapters * cap)
    pick = (slots[:, None] == row_slot[None, :]).astype(BF16)
    local = (row_adapter_index % held)[None, :] + 1
    ids = jnp.sum(jnp.where(slots[:, None] == row_slot[None, :], local, 0), axis=1) - 1
    ids = jnp.broadcast_to(ids[:, None], (adapters * cap, 128)).astype(BF16)
    place = (row_slot[:, None] == slots[None, :]).astype(BF16)

    quarter = width // tensors

    def quarters(array, parity):
        return jnp.concatenate(
            [lax.dynamic_slice_in_dim(array, (2 * i + parity) * quarter, quarter, 1) for i in range(2)], axis=1
        )

    gain = attention_norm_gain[None, :]
    lengths = jnp.broadcast_to(prompt_cache_length[:, None, None], (prompt_cache_length.shape[0], 8, 128))
    taken = lax.ppermute(quarters(partials[0], 1 - core), "tensor", swap_core)
    taken, pick, place, ids, gain, lengths = lax.optimization_barrier((taken, pick, place, ids, gain, lengths))
    chip_sum = (quarters(partials[0], core).astype(F32) + taken.astype(F32)).astype(BF16)
    other_sum = lax.ppermute(chip_sum, "tensor", swap_chip)
    flat_weight = key_value_weight.reshape(width, -1)
    flat_up = adapter_up_weight.reshape(adapter_up_weight.shape[0], -1)
    other_sum, flat_weight, flat_up = lax.optimization_barrier((other_sum, flat_weight, flat_up))
    near = (
        quarters(residual, core).astype(F32) + (chip_sum.astype(F32) + other_sum.astype(F32))
    ).astype(BF16)
    hidden_part = lax.dynamic_slice_in_dim(near, (t // 2) * quarter, quarter, 1)
    new_kv, attended = finish_rows(
        adapters, tensors, cap, near, gain, flat_weight, adapter_down_weight, key_value_cache, flat_up,
        pick, place, ids, queries, lengths,
    )
    return hidden_part, new_kv.reshape(rows, key_value_weight.shape[1], 2 * HEAD_SIZE), attended


def solution(mesh):
    return jax.shard_map(
        per_device,
        mesh=mesh,
        in_specs=(
            P("tensor", "adapter", None),
            P("adapter", None),
            P(),
            P(None, "tensor", None),
            P("tensor", "adapter"),
            P("adapter", "tensor", None),
            P("adapter"),
            P("adapter", "tensor"),
            P("adapter", None, None, "tensor"),
            P("adapter"),
        ),
        out_specs=(P("adapter", "tensor"), P("adapter", "tensor", None), P("adapter", "tensor")),
        check_vma=False,
    )
```
